256 devices in a mesh: dp: 8 (over z), expert: 32 (over y, x, core).
Axes of the slice: x: 4, y: 4, z: 8, core: 2. Of those that a mesh axis runs over, the one named last changes fastest.
Arguments:
- tokens: bfloat16 [40960, 2048], P(('dp', 'expert')), may hold values from -6 to 6
- expert_of: int32 [40960, 1], P(('dp', 'expert')), may hold values from 0 to 31; in each aligned block of 160 rows (0 to 159, 160 to 319, ...) at most 10 rows name the same one
- w_gate: bfloat16 [32, 2048, 768], P('expert'), may hold values from -0.125 to 0.125
- w_up: bfloat16 [32, 2048, 768], P('expert'), may hold values from -0.125 to 0.125
- w_down: bfloat16 [32, 768, 2048], P('expert'), may hold values from -0.21875 to 0.21875
- grad_out: bfloat16 [40960, 2048], P(('dp', 'expert')), may hold values from -6 to 6
Outputs:
- mixed: bfloat16 [40960, 2048], P(('dp', 'expert'))
- grad_tokens: bfloat16 [40960, 2048], P(('dp', 'expert'))
- grad_gate: bfloat16 [32, 2048, 768], P('expert', 'dp')
- grad_up: bfloat16 [32, 2048, 768], P('expert', 'dp')
- grad_down: bfloat16 [32, 768, 2048], P('expert', 'dp')
The draws below stay inside these ranges and needn't reach their ends.
Inputs may be any that keep to these rules, and one draw needn't show every extreme that they name: `expert_of`: within the rows of one device (aligned blocks of 160 rows) no expert is named by more than 10 rows, and in every draw some block names some expert exactly 10 times.
All inputs are finite; a program needn't handle non-finite values.
Results may differ from the reference program's by a relative error of at most 0.005.
Values may be sent and summed in bfloat16 or wider, within the bound.
No kernel may reach another device: no remote copies, remote signals or barrier semaphores. Data moves between devices by JAX's collectives and lax.ppermute only.
A program may use at most 128 MiB of HBM per device.

```python
import math
import jax
import jax.numpy as jnp
import numpy as np
from jax import lax

D = 2048
F = 768
TOK_DEV = 160
EXPERTS = 32
CAP = 10
TOKENS = 40960
SHARE = 1280
N_DP = 8
N_EXPERT = 32


def shard_levels(rng, dims, split, low, largest):
    def one(position, shards_of):
        steps = jax.random.uniform(jax.random.fold_in(jax.random.fold_in(rng, 6), position), (shards_of,), jnp.float32, low / len(split), largest / len(split))
        return jnp.repeat(jnp.exp(steps), dims[position] // shards_of).reshape((-1,) + (1,) * (len(dims) - position - 1))

    loudness = one(*split[0])
    for cut in split[1:]:
        loudness = loudness * one(*cut)
    return loudness


def deal_out(key, own, number, rows, number_of, top, bound, skew):
    ranking = jax.random.permutation(key, number_of)
    packed, common = shares(number_of, rows * top, bound, skew, True), shares(number_of, rows * top, bound, skew, False)
    places = jnp.arange(number_of)

    def named(tallies, offset_by):
        used = int((tallies > 0).sum())
        fixed = max(1, used // 4)
        moved = fixed + (places - fixed + offset_by * (used - fixed)) % max(1, number_of - fixed)
        return jnp.zeros((number_of,), jnp.int32).at[ranking[jnp.where(places < fixed, places, moved)]].set(jnp.asarray(tallies, jnp.int32))

    tallies = jnp.where(number % 4 == 0, named(packed, number // 4), named(common, number - number // 4 - 1))
    mixed = jax.random.permutation(jax.random.fold_in(own, 3), number_of)
    source_of, receiver = mixed[0:number_of // 2 * 2:2], mixed[1:number_of // 2 * 2:2]
    slack = jnp.minimum(tallies[source_of] - 1, bound - tallies[receiver]) // 2
    slack = jnp.where((source_of == ranking[0]) | (receiver == ranking[0]) | (tallies[receiver] == 0), 0, jnp.maximum(slack, 0))
    moved = jax.random.randint(jax.random.fold_in(own, 4), (number_of // 2,), 0, 1 << 20) % (slack + 1)
    tallies = tallies.at[source_of].add(-moved).at[receiver].add(moved)
    labels = jnp.searchsorted(jnp.cumsum(tallies), jnp.arange(rows * top), side="right").astype(jnp.int32)
    table = labels.reshape(top, rows).T
    table = table[jax.random.permutation(jax.random.fold_in(own, 1), rows)]
    offset_by = jax.random.randint(jax.random.fold_in(own, 2), (rows, 1), 0, top)
    return jnp.take_along_axis(table, (jnp.arange(top)[None, :] + offset_by) % top, axis=1)


def shares(number_of, total, reach, skew, full):
    weights = [(1 << 20) // math.isqrt(standing ** skew) + 1 for standing in range(1, number_of + 1)]
    largest = reach if full else min(reach, max(-(-total // number_of), total * weights[0] // sum(weights)))
    least = 1 if total - largest >= number_of - 1 else 0
    holding, rest = [largest] + [least] * (number_of - 1), total - largest - least * (number_of - 1)
    while rest > 0:
        candidates = [i for i in range(1, number_of) if holding[i] < largest] or [i for i in range(1, number_of) if holding[i] < reach]
        pool, left = sum([weights[i] for i in candidates]), rest
        for i in candidates:
            addition = min(reach - holding[i], max(1, left * weights[i] // pool), rest)
            holding[i] = holding[i] + addition
            rest = rest - addition
    return np.array(holding)


def gaussian(rng, dims, spread, bound, shards=(), kind=jnp.bfloat16):
    drawn = jax.random.normal(rng, dims, jnp.float32) * spread
    if len(shards) > 0:
        drawn = shard_levels(rng, dims, shards, -0.22, 0.18) * drawn
    return jnp.clip(drawn, min=-bound, max=bound).astype(kind)


def setup_inputs(seed: int = 0) -> dict:
    streams_of = jax.random.split(jax.random.key(seed), 7)
    tokens = gaussian(streams_of[0], (TOKENS, D), 1.0, 6.0, ((0, 256),))
    expert_of_keys = jax.random.split(jax.random.fold_in(streams_of[1], 1), TOKENS // TOK_DEV)
    expert_of_turns = jax.random.permutation(jax.random.fold_in(streams_of[1], 3), TOKENS // TOK_DEV)
    expert_of = jax.vmap(lambda own, number: deal_out(jax.random.fold_in(streams_of[1], 2), own, number, TOK_DEV, EXPERTS, 1, CAP, 2))(expert_of_keys, expert_of_turns).reshape((TOKENS, 1))
    w_gate = gaussian(streams_of[2], (EXPERTS, D, F), D ** -0.5, 0.125, ((0, 32),))
    w_up = gaussian(streams_of[3], (EXPERTS, D, F), D ** -0.5, 0.125, ((0, 32),))
    w_down = gaussian(streams_of[4], (EXPERTS, F, D), F ** -0.5, 0.21875, ((0, 32),))
    grad_out = gaussian(streams_of[5], (TOKENS, D), 1.0, 6.0, ((0, 256),))
    return dict(tokens=tokens, expert_of=expert_of, w_gate=w_gate, w_up=w_up, w_down=w_down, grad_out=grad_out)


def product(left, right):
    return jnp.dot(left, right, precision=lax.Precision.HIGHEST, preferred_element_type=jnp.float32)


def reference(tokens, expert_of, w_gate, w_up, w_down, grad_out):
    total = tokens.shape[0]
    width = tokens.shape[1]
    chosen = expert_of[:, 0].astype(jnp.int32)
    order = jnp.argsort(chosen, stable=True).astype(jnp.int32)
    counts = jnp.sum((chosen[:, None] == jnp.arange(EXPERTS, dtype=jnp.int32)[None, :]).astype(jnp.int32), axis=0)
    starts = (jnp.cumsum(counts) - counts).astype(jnp.int32)
    most = N_DP * N_EXPERT * CAP
    scale = float(SHARE) ** -0.5
    padding = jnp.zeros((most, width), jnp.float32)
    x_sorted = jnp.concatenate([tokens[order].astype(jnp.float32), padding], axis=0)
    dy_sorted = jnp.concatenate([grad_out[order].astype(jnp.float32), padding], axis=0)
    positions = jnp.arange(most, dtype=jnp.int32)

    def one_expert(carry, index):
        out_rows, grad_rows = carry
        begin = starts[index]
        live = (positions < counts[index])[:, None]
        x_rows = jnp.where(live, lax.dynamic_slice_in_dim(x_sorted, begin, most, 0), 0.0)
        dy_rows = jnp.where(live, lax.dynamic_slice_in_dim(dy_sorted, begin, most, 0), 0.0)
        gate_w = w_gate[index].astype(jnp.float32)
        up_w = w_up[index].astype(jnp.float32)
        down_w = w_down[index].astype(jnp.float32)
        gate_pre = product(x_rows, gate_w)
        up_pre = product(x_rows, up_w)
        swish = jax.nn.silu(gate_pre)
        act = lax.optimization_barrier((swish * up_pre).astype(jnp.bfloat16)).astype(jnp.float32)
        mixed_rows = product(act, down_w).astype(jnp.bfloat16)
        grad_act = product(dy_rows, down_w.T)
        sig = jax.nn.sigmoid(gate_pre)
        grad_gpre = lax.optimization_barrier((grad_act * up_pre * sig * (1.0 + gate_pre * (1.0 - sig))).astype(jnp.bfloat16)).astype(jnp.float32)
        grad_upre = lax.optimization_barrier((grad_act * swish).astype(jnp.bfloat16)).astype(jnp.float32)
        input_grad = (product(grad_gpre, gate_w.T) + product(grad_upre, up_w.T)).astype(jnp.bfloat16)
        gate_sum = (product(x_rows.T, grad_gpre) * scale).astype(jnp.bfloat16)
        up_sum = (product(x_rows.T, grad_upre) * scale).astype(jnp.bfloat16)
        down_sum = (product(act.T, dy_rows) * scale).astype(jnp.bfloat16)
        out_rows = lax.dynamic_update_slice_in_dim(out_rows, mixed_rows, begin, 0)
        grad_rows = lax.dynamic_update_slice_in_dim(grad_rows, input_grad, begin, 0)
        return (out_rows, grad_rows), (gate_sum, up_sum, down_sum)

    empty = jnp.zeros((total + most, width), jnp.bfloat16)
    (out_rows, grad_rows), (grad_gate, grad_up, grad_down) = lax.scan(one_expert, (empty, empty), jnp.arange(EXPERTS, dtype=jnp.int32))
    mixed = jnp.zeros((total, width), jnp.bfloat16).at[order].set(out_rows[:total])
    grad_tokens = jnp.zeros((total, width), jnp.bfloat16).at[order].set(grad_rows[:total])
    return mixed, grad_tokens, grad_gate, grad_up, grad_down
```

```python
import functools

import jax
import jax.numpy as jnp
from jax import lax
from jax.experimental import pallas as pl
from jax.experimental.pallas import tpu as pltpu
from jax.sharding import PartitionSpec as P

F32 = jnp.float32
BF16 = jnp.bfloat16
MAIN = 8
QUARTERS = 4
VMEM_LIMIT = 56 * 1024 * 1024


def mm(a, b, dims):
    return lax.dot_general(a, b, (dims, ((), ())), preferred_element_type=F32)


NN = ((1,), (0,))
NT = ((1,), (1,))
TN = ((0,), (0,))


def params():
    return pltpu.CompilerParams(vmem_limit_bytes=VMEM_LIMIT)


def iota(shape, dim):
    return lax.broadcasted_iota(jnp.int32, shape, dim)


def as_row(col):
    wide = jnp.broadcast_to(col.astype(F32), (col.shape[0], 128))
    return jnp.transpose(wide)[0:1, :].astype(jnp.int32)


def mask(cond):
    return jnp.where(cond, 1.0, 0.0).astype(BF16)


def pack_kernel(rows, width, peers, exp_ref, tok_ref, gout_ref, out_ref):
    col = exp_ref[...]
    row = as_row(col)
    earlier = (col == row) & (iota((rows, rows), 0) < iota((rows, rows), 1))
    rank = jnp.sum(jnp.where(earlier, 1.0, 0.0), axis=0, keepdims=True).astype(jnp.int32)
    slots = peers * MAIN
    r = iota((slots, rows), 0)
    here = (r >> 3) == row
    whole = mask(here & ((r & 7) == rank))
    late = here & (((r >> 2) & 1) + MAIN == rank)
    part = width // QUARTERS
    both = width + part
    for k, src in enumerate((tok_ref, gout_ref)):
        at = k * both
        out_ref[:, at : at + width] = mm(whole, src[...], NN).astype(BF16)
        tail = jnp.zeros((slots, part), F32)
        for q in range(QUARTERS):
            tail += mm(mask(late & ((r & 3) == q)), src[:, q * part : (q + 1) * part], NN)
        out_ref[:, at + width : at + both] = tail.astype(BF16)


def pack(expert_of, tokens, grad_out, peers):
    rows, width = tokens.shape
    return pl.pallas_call(
        functools.partial(pack_kernel, rows, width, peers),
        out_shape=jax.ShapeDtypeStruct((peers * MAIN, 2 * (width + width // QUARTERS)), BF16),
        compiler_params=params(),
        name="pack",
    )(expert_of, tokens, grad_out)


def unpack_kernel(rows, width, peers, exp_ref, back_ref, mixed_ref, gtok_ref):
    col = exp_ref[...]
    row = as_row(col)
    earlier = (col == row) & (iota((rows, rows), 1) < iota((rows, rows), 0))
    rank = jnp.sum(jnp.where(earlier, 1.0, 0.0), axis=1, keepdims=True).astype(jnp.int32)
    slots = peers * MAIN
    r = iota((rows, slots), 1)
    here = (r >> 3) == col
    whole = mask(here & ((r & 7) == rank))
    late = here & (((r >> 2) & 1) + MAIN == rank)
    part = width // QUARTERS
    both = width + part
    for k, dst in enumerate((mixed_ref, gtok_ref)):
        at = k * both
        tail = back_ref[:, at + width : at + both]
        for q in range(QUARTERS):
            got = mm(whole, back_ref[:, at + q * part : at + (q + 1) * part], NN)
            got += mm(mask(late & ((r & 3) == q)), tail, NN)
            dst[:, q * part : (q + 1) * part] = got.astype(BF16)


def unpack(expert_of, back, rows, width, peers):
    out = jax.ShapeDtypeStruct((rows, width), BF16)
    return pl.pallas_call(
        functools.partial(unpack_kernel, rows, width, peers),
        out_shape=(out, out),
        compiler_params=params(),
        name="unpack",
    )(expert_of, back)


def picks(slots, tails, q):
    return mask(iota((tails, slots), 1) == iota((tails, slots), 0) * QUARTERS + q)


def hidden_kernel(scale, recv_ref, wg_ref, wu_ref, wd_ref, x_ref, act_ref, gg_ref, gu_ref, down_ref, dy_ref):
    slots = recv_ref.shape[0]
    width = x_ref.shape[1]
    part = width // QUARTERS
    tails = slots // QUARTERS

    @pl.when(pl.program_id(0) == 0)
    def _():
        for k, dst in enumerate((x_ref, dy_ref)):
            at = k * (width + part)
            dst[0:slots, :] = recv_ref[:, at : at + width]
            tail = recv_ref[:, at + width : at + width + part]
            for q in range(QUARTERS):
                dst[slots : slots + tails, q * part : (q + 1) * part] = mm(
                    picks(slots, tails, q), tail, NN
                ).astype(BF16)

    x = x_ref[...]
    dy = dy_ref[...]
    gate = mm(x, wg_ref[...], NN)
    up = mm(x, wu_ref[...], NN)
    sig = jax.nn.sigmoid(gate)
    swish = gate * sig
    act = (swish * up).astype(BF16)
    act_ref[...] = act
    down_ref[...] = (mm(act, dy, TN) * scale).astype(BF16)
    grad_act = mm(dy, wd_ref[...], NT)
    gg_ref[...] = (grad_act * up * sig * (1.0 + gate * (1.0 - sig))).astype(BF16)
    gu_ref[...] = (grad_act * swish).astype(BF16)


def hidden(recv, wg, wu, wd, scale, tile=256):
    slots = recv.shape[0]
    width, inner = wg.shape
    total = slots + slots // QUARTERS
    cols = pl.BlockSpec((width, tile), lambda i: (0, i))
    rows = pl.BlockSpec((tile, width), lambda i: (i, 0))
    slab = pl.BlockSpec((total, tile), lambda i: (0, i))
    mid = jax.ShapeDtypeStruct((total, inner), BF16)
    return pl.pallas_call(
        functools.partial(hidden_kernel, scale),
        grid=(inner // tile,),
        in_specs=[pl.BlockSpec(recv.shape, lambda i: (0, 0)), cols, cols, rows],
        out_specs=[pl.BlockSpec((total, width), lambda i: (0, 0)), slab, slab, slab, rows],
        out_shape=[
            jax.ShapeDtypeStruct((total, width), BF16),
            mid,
            mid,
            mid,
            jax.ShapeDtypeStruct((inner, width), BF16),
        ],
        scratch_shapes=[pltpu.VMEM((total, width), BF16)],
        compiler_params=params(),
        cost_estimate=pl.CostEstimate(
            flops=8 * total * width * inner, bytes_accessed=8 * width * inner, transcendentals=total * inner
        ),
        name="hidden",
    )(recv, wg, wu, wd)


def outer_kernel(scale, x_ref, gg_ref, gu_ref, gate_ref, up_ref):
    x = x_ref[...]
    gate_ref[0] = (mm(x, gg_ref[...], TN) * scale).astype(BF16)
    up_ref[0] = (mm(x, gu_ref[...], TN) * scale).astype(BF16)


def outer(x, gg, gu, scale, groups):
    total, width = x.shape
    inner = gg.shape[1]
    rows = width // groups
    whole = pl.BlockSpec((total, inner), lambda i: (0, 0))
    piece = pl.BlockSpec((1, rows, inner), lambda i: (i, 0, 0))
    out = jax.ShapeDtypeStruct((groups, rows, inner), BF16)
    return pl.pallas_call(
        functools.partial(outer_kernel, scale),
        grid=(groups,),
        in_specs=[pl.BlockSpec((total, rows), lambda i: (0, i)), whole, whole],
        out_specs=[piece, piece],
        out_shape=[out, out],
        compiler_params=params(),
        cost_estimate=pl.CostEstimate(
            flops=4 * total * width * inner, bytes_accessed=4 * width * inner, transcendentals=0
        ),
        name="outer",
    )(x, gg, gu)


def rows_kernel(act_ref, gg_ref, gu_ref, wg_ref, wu_ref, wd_ref, out_ref):
    step = pl.program_id(0)
    slots = out_ref.shape[0]
    part = wd_ref.shape[1]
    width = part * QUARTERS
    both = width + part
    tails = slots // QUARTERS
    mixed = mm(act_ref[...], wd_ref[...], NN).astype(BF16)
    gtok = (mm(gg_ref[...], wg_ref[...], NT) + mm(gu_ref[...], wu_ref[...], NT)).astype(BF16)
    pick = mask(iota((slots, tails), 0) == iota((slots, tails), 1) * QUARTERS + step)
    mine = (iota((slots, part), 0) & (QUARTERS - 1)) == step
    for k, val in enumerate((mixed, gtok)):
        at = pl.multiple_of(k * both + step * part, 128)
        out_ref[:, pl.ds(at, part)] = val[0:slots, :]
        tail = mm(pick, val[slots : slots + tails, :], NN).astype(BF16)
        lo = k * both + width
        out_ref[:, lo : lo + part] = jnp.where(mine, tail, out_ref[:, lo : lo + part])


def rows_back(act, gg, gu, wg, wu, wd):
    total, inner = act.shape
    width = wg.shape[0]
    slots = total * QUARTERS // (QUARTERS + 1)
    part = width // QUARTERS
    whole = pl.BlockSpec((total, inner), lambda i: (0, 0))
    wrow = pl.BlockSpec((part, inner), lambda i: (i, 0))
    out = (slots, 2 * (width + part))
    return pl.pallas_call(
        rows_kernel,
        grid=(QUARTERS,),
        in_specs=[whole, whole, whole, wrow, wrow, pl.BlockSpec((inner, part), lambda i: (0, i))],
        out_specs=pl.BlockSpec(out, lambda i: (0, 0)),
        out_shape=jax.ShapeDtypeStruct(out, BF16),
        compiler_params=params(),
        cost_estimate=pl.CostEstimate(
            flops=6 * total * width * inner, bytes_accessed=6 * width * inner, transcendentals=0
        ),
        name="rows_back",
    )(act, gg, gu, wg, wu, wd)


def ring_sums(tensors):
    groups = tensors[0].shape[0]
    z = lax.axis_index("dp")
    right = [(i, (i + 1) % groups) for i in range(groups)]
    left = [(i, (i - 1) % groups) for i in range(groups)]

    def own(parts, d):
        return lax.dynamic_index_in_dim(parts, (z + d) % groups, 0, keepdims=False)

    def add(a, b):
        return (a.astype(F32) + b.astype(F32)).astype(BF16)

    def send(r, l):
        return lax.ppermute(r, "dp", right), lax.ppermute(l, "dp", left)

    far = groups // 2
    halves = [parts.shape[1] // 2 for parts in tensors]
    moving = [send(own(p, far)[:h], own(p, far)[h:]) for p, h in zip(tensors, halves)]
    for d in range(far - 1, 0, -1):
        for k, (p, h) in enumerate(zip(tensors, halves)):
            r, l = moving[k]
            a, b = own(p, d), own(p, -d)
            if d == far - 1:
                r = jnp.concatenate([add(a[:h], r), a[h:]], 0)
                l = jnp.concatenate([b[:h], add(b[h:], l)], 0)
            else:
                r, l = add(a, r), add(b, l)
            moving[k] = send(r, l)
    return [
        (own(p, 0).astype(F32) + r.astype(F32) + l.astype(F32)).astype(BF16)
        for p, (r, l) in zip(tensors, moving)
    ]


def shards(tokens, expert_of, w_gate, w_up, w_down, grad_out):
    rows, width = tokens.shape
    peers = lax.axis_size("expert")
    groups = lax.axis_size("dp")
    wg, wu, wd = w_gate[0], w_up[0], w_down[0]
    inner = wg.shape[1]
    scale = float(rows * groups) ** (-0.5)

    def exchange(packed):
        swapped = lax.all_to_all(
            packed.reshape(peers, MAIN, -1), "expert", split_axis=0, concat_axis=0, tiled=True
        )
        return swapped.reshape(peers * MAIN, -1)

    recv = exchange(pack(expert_of, tokens, grad_out, peers))
    x, act, gg, gu, down = hidden(recv, wg, wu, wd, scale)
    gate, up = outer(x, gg, gu, scale, groups)
    grad_down, grad_gate, grad_up = ring_sums([down.reshape(groups, inner // groups, width), gate, up])
    back = exchange(rows_back(act, gg, gu, wg, wu, wd))
    mixed, grad_tokens = unpack(expert_of, back, rows, width, peers)
    return mixed, grad_tokens, grad_gate[None], grad_up[None], grad_down[None]


def solution(mesh):
    in_specs = (
        P(("dp", "expert"), None),
        P(("dp", "expert"), None),
        P("expert", None, None),
        P("expert", None, None),
        P("expert", None, None),
        P(("dp", "expert"), None),
    )
    out_specs = (
        P(("dp", "expert"), None),
        P(("dp", "expert"), None),
        P("expert", "dp", None),
        P("expert", "dp", None),
        P("expert", "dp", None),
    )
    return jax.shard_map(shards, mesh=mesh, in_specs=in_specs, out_specs=out_specs, check_vma=False)
```

```python
import functools

import jax
import jax.numpy as jnp
from jax import lax
from jax.experimental import pallas as pl
from jax.experimental.pallas import tpu as pltpu
from jax.sharding import PartitionSpec as P

F32 = jnp.float32
BF16 = jnp.bfloat16
MAIN = 8
QUARTERS = 4
LANES = 256
MIB = 1024 * 1024
FREE = pl.CostEstimate(flops=0, bytes_accessed=0, transcendentals=0)


def mm(a, b, dims):
    return lax.dot_general(a, b, (dims, ((), ())), preferred_element_type=F32)


NN = ((1,), (0,))
NT = ((1,), (1,))
TN = ((0,), (0,))


def params(mib):
    return pltpu.CompilerParams(vmem_limit_bytes=mib * MIB)


def iota(shape, dim):
    return lax.broadcasted_iota(jnp.int32, shape, dim)


def as_col(row):
    tall = jnp.broadcast_to(row.astype(F32), (128, row.shape[1]))
    return jnp.transpose(tall)[:, 0:1].astype(jnp.int32)


def in_hbm(x):
    return pltpu.with_memory_space_constraint(x, pltpu.HBM)


def mask(cond):
    return jnp.where(cond, 1.0, 0.0).astype(BF16)


def pack_kernel(rows, peers, exp_hbm, tok_hbm, gout_hbm, out_hbm, exp_ref, src, out, sem_exp, sem_in, sem_out):
    expert = pltpu.make_async_copy(exp_hbm, exp_ref, sem_exp)
    expert.start()
    width = tok_hbm.shape[1]
    part = width // QUARTERS
    both = width + part
    loads = []
    for k, hbm in enumerate((tok_hbm, gout_hbm)):
        for q in range(QUARTERS):
            cols = pl.ds(q * part, part)
            copy = pltpu.make_async_copy(hbm.at[:, cols], src.at[k, :, cols], sem_in.at[k * QUARTERS + q])
            copy.start()
            loads.append(copy)
    expert.wait()
    row = exp_ref[...]
    earlier = (as_col(row) == row) & (iota((rows, rows), 0) < iota((rows, rows), 1))
    rank = jnp.sum(jnp.where(earlier, 1.0, 0.0), axis=0, keepdims=True).astype(jnp.int32)
    slots = peers * MAIN
    r = iota((slots, rows), 0)
    here = (r >> 3) == row
    whole = mask(here & ((r & 7) == rank))
    late = here & (((r >> 2) & 1) + MAIN == rank)
    late = [mask(late & ((r & 3) == q)) for q in range(QUARTERS)]
    stores = []

    def store(lo, size):
        cols = pl.ds(lo, size)
        copy = pltpu.make_async_copy(out.at[:, cols], out_hbm.at[:, cols], sem_out.at[len(stores)])
        copy.start()
        stores.append(copy)

    for k in range(2):
        at = k * both
        tail = jnp.zeros((slots, part), F32)
        for q in range(QUARTERS):
            loads[k * QUARTERS + q].wait()
            cols = src[k, :, q * part : (q + 1) * part]
            out[:, at + q * part : at + (q + 1) * part] = mm(whole, cols, NN).astype(BF16)
            store(at + q * part, part)
            tail += mm(late[q], cols, NN)
        out[:, at + width : at + both] = tail.astype(BF16)
        store(at + width, part)
    for copy in stores:
        copy.wait()


def pack(expert_row, tokens, grad_out, peers):
    rows, width = tokens.shape
    both = width + width // QUARTERS
    slots = peers * MAIN
    hbm = pl.BlockSpec(memory_space=pltpu.HBM)
    return pl.pallas_call(
        functools.partial(pack_kernel, rows, peers),
        in_specs=[hbm, hbm, hbm],
        out_specs=hbm,
        out_shape=pltpu.HBM((slots, 2 * both), BF16),
        scratch_shapes=[
            pltpu.VMEM((1, rows), jnp.int32),
            pltpu.VMEM((2, rows, width), BF16),
            pltpu.VMEM((slots, 2 * both), BF16),
            pltpu.SemaphoreType.DMA,
            pltpu.SemaphoreType.DMA((2 * QUARTERS,)),
            pltpu.SemaphoreType.DMA((2 * QUARTERS + 2,)),
        ],
        compiler_params=params(12),
        cost_estimate=FREE,
        name="pack",
    )(in_hbm(expert_row), in_hbm(tokens), in_hbm(grad_out))


def fetch_kernel(src, dst, sem):
    copy = pltpu.make_async_copy(src, dst, sem)
    copy.start()
    copy.wait()


def fetch(array):
    return pl.pallas_call(
        fetch_kernel,
        in_specs=[pl.BlockSpec(memory_space=pltpu.HBM)],
        out_specs=pl.BlockSpec(memory_space=pltpu.VMEM),
        out_shape=pltpu.VMEM(array.shape, array.dtype),
        scratch_shapes=[pltpu.SemaphoreType.DMA],
        compiler_params=params(2),
        cost_estimate=FREE,
        name="fetch",
    )(in_hbm(array))


def unpack_kernel(rows, peers, exp_ref, back_ref, mixed_ref, gtok_ref):
    row = exp_ref[...]
    col = as_col(row)
    earlier = (col == row) & (iota((rows, rows), 1) < iota((rows, rows), 0))
    rank = jnp.sum(jnp.where(earlier, 1.0, 0.0), axis=1, keepdims=True).astype(jnp.int32)
    slots = peers * MAIN
    r = iota((rows, slots), 1)
    here = (r >> 3) == col
    whole = mask(here & ((r & 7) == rank))
    late = here & (((r >> 2) & 1) + MAIN == rank)
    part = mixed_ref.shape[1] // QUARTERS
    both = part * (QUARTERS + 1)
    for k, dst in enumerate((mixed_ref, gtok_ref)):
        at = k * both
        tail = back_ref[:, at + QUARTERS * part : at + both]
        for q in range(QUARTERS):
            got = mm(whole, back_ref[:, at + q * part : at + (q + 1) * part], NN)
            got += mm(mask(late & ((r & 3) == q)), tail, NN)
            dst[:, q * part : (q + 1) * part] = got.astype(BF16)


def unpack(expert_row, back, width, peers):
    rows = expert_row.shape[1]
    out = jax.ShapeDtypeStruct((rows, width), BF16)
    return pl.pallas_call(
        functools.partial(unpack_kernel, rows, peers),
        out_shape=(out, out),
        compiler_params=params(12),
        cost_estimate=FREE,
        name="unpack",
    )(expert_row, back)


def grad_block(groups, scale, z, x_ref, dy_ref, cut_ref, gg_ref, gu_ref, a_ref, b_ref):
    rows = x_ref.shape[1] // groups
    half = rows // 2
    at = z % groups
    x = x_ref[:, pl.ds(pl.multiple_of(at * rows, 128), rows)]

    def put(ref, base, value):
        n = value.shape[0]
        for c in range(value.shape[1] // LANES):
            ref[base + c * n : base + (c + 1) * n, :] = value[:, c * LANES : (c + 1) * LANES]
        return base + n * (value.shape[1] // LANES)

    if a_ref is not None and b_ref is not None:
        up = (mm(x, gu_ref[...], TN) * scale).astype(BF16)
        upper, lower = up[:half], up[half:]
    elif a_ref is not None:
        upper = (mm(x[:, :half], gu_ref[...], TN) * scale).astype(BF16)
    else:
        lower = (mm(x[:, half:], gu_ref[...], TN) * scale).astype(BF16)
    if a_ref is not None:
        down = (mm(cut_ref[at], dy_ref[...], TN) * scale).astype(BF16)
        put(a_ref, put(a_ref, 0, down), upper)
    if b_ref is not None:
        gate = (mm(x, gg_ref[...], TN) * scale).astype(BF16)
        put(b_ref, put(b_ref, 0, gate), lower)


def hidden_kernel(
    groups, tile, scale, z_ref, recv_hbm, wg_ref, wu_hbm, wd_hbm,
    x_ref, dy_ref, act_ref, cut_ref, gg_ref, gu_ref, a4, b4, b3, a5,
    recv_ref, wu_ref, wd_ref, gate_ref, up_ref, sem_x, sem_dy, sem_u, sem_d,
):
    slots = recv_ref.shape[0]
    width, inner = wg_ref.shape
    part = width // QUARTERS
    both = width + part
    tails = slots // QUARTERS
    tiles = [slice(lo, lo + tile) for lo in range(0, inner, tile)]
    halves = [(slice(None), slice(0, both)), (slice(None), slice(both, 2 * both))]
    load_x = pltpu.make_async_copy(recv_hbm.at[halves[0]], recv_ref.at[halves[0]], sem_x)
    load_dy = pltpu.make_async_copy(recv_hbm.at[halves[1]], recv_ref.at[halves[1]], sem_dy)
    load_u = pltpu.make_async_copy(wu_hbm, wu_ref, sem_u)
    load_d = pltpu.make_async_copy(wd_hbm, wd_ref, sem_d)
    load_x.start()
    load_u.start()
    load_dy.start()
    load_d.start()
    picks = [
        mask(iota((tails, slots), 1) == iota((tails, slots), 0) * QUARTERS + q) for q in range(QUARTERS)
    ]

    def spread(k, dst):
        at = k * both
        dst[0:slots, :] = recv_ref[:, at : at + width]
        tail = recv_ref[:, at + width : at + both]
        for q in range(QUARTERS):
            dst[slots : slots + tails, q * part : (q + 1) * part] = mm(picks[q], tail, NN).astype(BF16)

    load_x.wait()
    spread(0, x_ref)
    for cols in tiles:
        gate_ref[:, cols] = mm(x_ref[...], wg_ref[:, cols], NN)
    load_u.wait()
    for cols in tiles:
        up_ref[:, cols] = mm(x_ref[...], wu_ref[:, cols], NN)
    load_dy.wait()
    spread(1, dy_ref)
    load_d.wait()
    for cols in tiles:
        gate, up = gate_ref[:, cols], up_ref[:, cols]
        grad_act = mm(dy_ref[...], wd_ref[cols, :], NT)
        sig = jax.nn.sigmoid(gate)
        swish = gate * sig
        act_ref[:, cols] = (swish * up).astype(BF16)
        gg_ref[:, cols] = (grad_act * up * sig * (1.0 + gate * (1.0 - sig))).astype(BF16)
        gu_ref[:, cols] = (grad_act * swish).astype(BF16)
    each = inner // groups
    for k in range(groups):
        cut_ref[k] = act_ref[:, k * each : (k + 1) * each]
    far = groups // 2
    for d, a_ref, b_ref in ((far, a4, b4), (far - 1, None, b3), (far + 1, a5, None)):
        grad_block(groups, scale, z_ref[0] + d, x_ref, dy_ref, cut_ref, gg_ref, gu_ref, a_ref, b_ref)


def hidden(z, recv, wg, wu, wd, scale, groups, tile=256):
    slots = recv.shape[0]
    width, inner = wg.shape
    total = slots + slots // QUARTERS
    shapes = [(total, width)] * 2 + [(total, inner), (groups, total, inner // groups)] + [(total, inner)] * 2
    shapes += [(3 * width * inner // (2 * groups * LANES), LANES)] * 4
    vmem = pl.BlockSpec(memory_space=pltpu.VMEM)
    hbm = pl.BlockSpec(memory_space=pltpu.HBM)
    return pl.pallas_call(
        functools.partial(hidden_kernel, groups, tile, scale),
        in_specs=[pl.BlockSpec(memory_space=pltpu.SMEM), hbm, vmem, hbm, hbm],
        out_specs=[vmem] * len(shapes),
        out_shape=[jax.ShapeDtypeStruct(s, BF16) for s in shapes],
        scratch_shapes=[
            pltpu.VMEM(recv.shape, BF16),
            pltpu.VMEM(wu.shape, BF16),
            pltpu.VMEM(wd.shape, BF16),
            pltpu.VMEM((total, inner), F32),
            pltpu.VMEM((total, inner), F32),
        ]
        + [pltpu.SemaphoreType.DMA] * 4,
        compiler_params=params(24),
        cost_estimate=pl.CostEstimate(
            flops=6 * total * width * inner, bytes_accessed=8 * width * inner, transcendentals=total * inner
        ),
        name="hidden",
    )(z, in_hbm(recv), wg, in_hbm(wu), in_hbm(wd))


def near_kernel(groups, scale, z_ref, cut_ref, x_ref, dy_ref, gg_ref, gu_ref, *refs):
    count = groups - 1
    outs, (a_ref, b_ref, sems) = refs[: 2 * (count - 1)], refs[2 * (count - 1) :]
    copies = []
    for i in range(count):
        z = z_ref[0] + groups // 2 + 1 + i
        a = a_ref.at[i] if i > 0 else None
        b = b_ref.at[i] if i < count - 1 else None
        grad_block(groups, scale, z, x_ref, dy_ref, cut_ref, gg_ref, gu_ref, a, b)
        for ref, out in ((a, i - 1), (b, count - 1 + i)):
            if ref is not None:
                copies.append(pltpu.make_async_copy(ref, outs[out], sems.at[len(copies)]))
                copies[-1].start()
    for copy in copies:
        copy.wait()


def near_blocks(z, cut, x, dy, gg, gu, scale):
    groups, total, each = cut.shape
    width = x.shape[1]
    inner = gg.shape[1]
    vmem = pl.BlockSpec(memory_space=pltpu.VMEM)
    hbm = pl.BlockSpec(memory_space=pltpu.HBM)
    one = (3 * width * inner // (2 * groups * LANES), LANES)
    count = 2 * (groups - 2)
    outs = pl.pallas_call(
        functools.partial(near_kernel, groups, scale),
        in_specs=[pl.BlockSpec(memory_space=pltpu.SMEM)] + [vmem] * 5,
        out_specs=[hbm] * count,
        out_shape=[pltpu.HBM(one, BF16)] * count,
        scratch_shapes=[pltpu.VMEM((groups - 1, *one), BF16)] * 2 + [pltpu.SemaphoreType.DMA((count,))],
        compiler_params=params(16),
        cost_estimate=pl.CostEstimate(
            flops=6 * total * width * inner, bytes_accessed=6 * width * inner, transcendentals=0
        ),
        name="near_blocks",
    )(z, cut, x, dy, gg, gu)
    far = groups // 2
    a = {d: outs[d + far - 2] for d in range(2 - far, far)}
    b = {d: outs[groups - 2 + d + far - 1] for d in range(1 - far, far - 1)}
    return a, b


def almost_kernel(own_a, own_b, al_any, br_any, pa, pb, oa, ob, al, br, sems):
    pairs = ((own_a, oa), (al_any, al), (own_b, ob), (br_any, br))
    loads = [pltpu.make_async_copy(src, dst, sems.at[n]) for n, (src, dst) in enumerate(pairs)]
    for copy in loads:
        copy.start()
    for copy in loads:
        copy.wait()
    pa[...] = oa[...].astype(F32) + al[...].astype(F32)
    pb[...] = ob[...].astype(F32) + br[...].astype(F32)


def almost(own_a, own_b, al, br):
    vmem = pl.BlockSpec(memory_space=pltpu.VMEM)
    return pl.pallas_call(
        almost_kernel,
        in_specs=[pl.BlockSpec(memory_space=pl.ANY)] * 4,
        out_specs=[vmem] * 2,
        out_shape=[pltpu.VMEM(al.shape, F32)] * 2,
        scratch_shapes=[pltpu.VMEM(al.shape, BF16)] * 4 + [pltpu.SemaphoreType.DMA((4,))],
        compiler_params=params(6),
        cost_estimate=FREE,
        name="almost",
    )(in_hbm(own_a), in_hbm(own_b), al, br)


def finish_kernel(after, pa, pb, ar_any, bl_any, down_hbm, gate_hbm, up_hbm, ar, bl, down, gate, up, sem_in, sem_out):
    loads = [
        pltpu.make_async_copy(src, dst, sem_in.at[n]) for n, (src, dst) in enumerate(((ar_any, ar), (bl_any, bl)))
    ]
    for copy in loads:
        copy.start()
    half = up.shape[0] // 2
    stores = []

    def take(part, moved, base, dst):
        rows = dst.shape[0]
        for c in range(dst.shape[1] // LANES):
            at = slice(base + c * rows, base + (c + 1) * rows)
            dst[:, c * LANES : (c + 1) * LANES] = (part[at, :] + moved[at, :].astype(F32)).astype(BF16)
        return base + rows * (dst.shape[1] // LANES)

    def store(src, dst):
        stores.append(pltpu.make_async_copy(src, dst, sem_out.at[len(stores)]))
        stores[-1].start()

    loads[0].wait()
    base = take(pa, ar, 0, down)
    store(down, down_hbm)
    take(pa, ar, base, up.at[:half])
    store(up.at[:half], up_hbm.at[:half])
    loads[1].wait()
    base = take(pb, bl, 0, gate)
    store(gate, gate_hbm)
    take(pb, bl, base, up.at[half:])
    store(up.at[half:], up_hbm.at[half:])
    for copy in stores:
        copy.wait()


def finish(after, sums, ar, bl, groups, width, inner):
    vmem = pl.BlockSpec(memory_space=pltpu.VMEM)
    hbm = pl.BlockSpec(memory_space=pltpu.HBM)
    anywhere = pl.BlockSpec(memory_space=pl.ANY)
    shapes = [(inner // groups, width), (width // groups, inner), (width // groups, inner)]
    return pl.pallas_call(
        finish_kernel,
        in_specs=[anywhere, vmem, vmem, anywhere, anywhere],
        out_specs=[hbm] * 3,
        out_shape=[pltpu.HBM(s, BF16) for s in shapes],
        scratch_shapes=[pltpu.VMEM(ar.shape, BF16)] * 2
        + [pltpu.VMEM(s, BF16) for s in shapes]
        + [pltpu.SemaphoreType.DMA((2,)), pltpu.SemaphoreType.DMA((4,))],
        compiler_params=params(6),
        cost_estimate=FREE,
        name="finish",
    )(in_hbm(after), *sums, ar, bl)


def rows_kernel(
    after, act_ref, gg_ref, gu_ref, wg_hbm, wu_hbm, wd_hbm, out_hbm, wg_ref, wu_ref, wd_ref, out, sem_in, sem_out
):
    slots = out.shape[0]
    width = wg_ref.shape[0]
    part = width // QUARTERS
    both = width + part
    tails = slots // QUARTERS
    loads = []
    for q in range(QUARTERS):
        cut = slice(q * part, (q + 1) * part)
        where = ((wd_hbm, wd_ref, (slice(None), cut)), (wg_hbm, wg_ref, (cut,)), (wu_hbm, wu_ref, (cut,)))
        for n, (src, dst, at) in enumerate(where):
            copy = pltpu.make_async_copy(src.at[at], dst.at[at], sem_in.at[q * 3 + n])
            copy.start()
            loads.append(copy)
    stores = []

    def store(lo):
        cols = pl.ds(lo, part)
        copy = pltpu.make_async_copy(out.at[:, cols], out_hbm.at[:, cols], sem_out.at[len(stores)])
        copy.start()
        stores.append(copy)

    tail = [jnp.zeros((slots, part), F32) for _ in range(2)]
    for q in range(QUARTERS):
        cut = slice(q * part, (q + 1) * part)
        pick = mask(iota((slots, tails), 0) == iota((slots, tails), 1) * QUARTERS + q)
        for k in range(2):
            if k == 0:
                loads[q * 3].wait()
                val = mm(act_ref[...], wd_ref[:, cut], NN).astype(BF16)
            else:
                loads[q * 3 + 1].wait()
                loads[q * 3 + 2].wait()
                val = (mm(gg_ref[...], wg_ref[cut, :], NT) + mm(gu_ref[...], wu_ref[cut, :], NT)).astype(BF16)
            lo = k * both + q * part
            out[:, lo : lo + part] = val[0:slots, :]
            store(lo)
            tail[k] += mm(pick, val[slots : slots + tails, :], NN)
    for k in range(2):
        lo = k * both + width
        out[:, lo : lo + part] = tail[k].astype(BF16)
        store(lo)
    for copy in stores:
        copy.wait()


def rows_back(after, act, gg, gu, wg, wu, wd):
    total, inner = act.shape
    width = wg.shape[0]
    slots = total * QUARTERS // (QUARTERS + 1)
    out = (slots, 2 * (width + width // QUARTERS))
    vmem = pl.BlockSpec(memory_space=pltpu.VMEM)
    hbm = pl.BlockSpec(memory_space=pltpu.HBM)
    return pl.pallas_call(
        rows_kernel,
        in_specs=[pl.BlockSpec(memory_space=pl.ANY), vmem, vmem, vmem, hbm, hbm, hbm],
        out_specs=hbm,
        out_shape=pltpu.HBM(out, BF16),
        scratch_shapes=[
            pltpu.VMEM(wg.shape, BF16),
            pltpu.VMEM(wu.shape, BF16),
            pltpu.VMEM(wd.shape, BF16),
            pltpu.VMEM(out, BF16),
            pltpu.SemaphoreType.DMA((3 * QUARTERS,)),
            pltpu.SemaphoreType.DMA((2 * QUARTERS + 2,)),
        ],
        compiler_params=params(20),
        cost_estimate=pl.CostEstimate(
            flops=6 * total * width * inner, bytes_accessed=6 * width * inner, transcendentals=0
        ),
        name="rows_back",
    )(in_hbm(after), act, gg, gu, in_hbm(wg), in_hbm(wu), in_hbm(wd))


def step_kernel(after, own_r, own_l, r_any, l_any, out_r, out_l, o_r, o_l, r, l, sems):
    pairs = ((own_r, o_r), (r_any, r), (own_l, o_l), (l_any, l))
    loads = [pltpu.make_async_copy(src, dst, sems.at[n]) for n, (src, dst) in enumerate(pairs)]
    for copy in loads:
        copy.start()
    stores = []
    for n, (own, moved, out) in enumerate(((o_r, r, out_r), (o_l, l, out_l))):
        for copy in loads[2 * n : 2 * n + 2]:
            copy.wait()
        own[...] = (own[...].astype(F32) + moved[...].astype(F32)).astype(BF16)
        stores.append(pltpu.make_async_copy(own, out, sems.at[4 + n]))
        stores[n].start()
    for copy in stores:
        copy.wait()


def ring_step(after, own_r, own_l, r, l):
    hbm = pl.BlockSpec(memory_space=pltpu.HBM)
    return pl.pallas_call(
        step_kernel,
        in_specs=[pl.BlockSpec(memory_space=pl.ANY)] * 5,
        out_specs=[hbm] * 2,
        out_shape=[pltpu.HBM(r.shape, BF16)] * 2,
        scratch_shapes=[pltpu.VMEM(r.shape, BF16)] * 4 + [pltpu.SemaphoreType.DMA((6,))],
        compiler_params=params(6),
        cost_estimate=FREE,
        name="ring_step",
    )(in_hbm(after), in_hbm(own_r), in_hbm(own_l), r, l)


def ring_sums(first, rest, groups):
    right = [(i, (i + 1) % groups) for i in range(groups)]
    left = [(i, (i - 1) % groups) for i in range(groups)]
    far = groups // 2
    send = lambda r, l: (lax.ppermute(r, "dp", right), lax.ppermute(l, "dp", left))
    a4, b4, b3, a5 = first
    a, b = 0, 1
    moving = [send(a4, b4), send(b3, a5)]
    after = None
    for n in range(2, 2 * far - 1):
        i, j = (a, b) if n % 2 == 0 else (b, a)
        d = far - (n + 1) // 2
        r, l = moving[n - 2]
        after = ring_step(rest[a][0] if after is None else after[0], rest[i][d], rest[j][-d], r, l)
        moving.append(send(*after))
    br, al = moving[-2]
    return almost(rest[a][0], rest[b][0], al, br), *moving[-1]


def shards(tokens, expert_of, w_gate, w_up, w_down, grad_out):
    rows, width = tokens.shape
    peers = lax.axis_size("expert")
    groups = lax.axis_size("dp")
    wg, wu, wd = w_gate[0], w_up[0], w_down[0]
    scale = float(rows * groups) ** (-0.5)

    def exchange(packed):
        swapped = lax.all_to_all(
            packed.reshape(peers, MAIN, -1), "expert", split_axis=0, concat_axis=0, tiled=True
        )
        return swapped.reshape(peers * MAIN, -1)

    expert_row = expert_of.reshape(1, rows)
    z = lax.axis_index("dp").astype(jnp.int32).reshape(1)
    recv = exchange(pack(expert_row, tokens, grad_out, peers))
    x, dy, act, cut, gg, gu, *first = hidden(z, recv, fetch(wg), wu, wd, scale, groups)
    rest = near_blocks(z, cut, x, dy, gg, gu, scale)
    back = exchange(rows_back(rest[0][0], act, gg, gu, wg, wu, wd))
    sums, ar, bl = ring_sums(first, rest, groups)
    mixed, grad_tokens = unpack(expert_row, back, width, peers)
    grad_down, grad_gate, grad_up = finish(mixed, sums, ar, bl, groups, width, wg.shape[1])
    return mixed, grad_tokens, grad_gate[None], grad_up[None], grad_down[None]


def solution(mesh):
    in_specs = (
        P(("dp", "expert"), None),
        P(("dp", "expert"), None),
        P("expert", None, None),
        P("expert", None, None),
        P("expert", None, None),
        P(("dp", "expert"), None),
    )
    out_specs = (
        P(("dp", "expert"), None),
        P(("dp", "expert"), None),
        P("expert", "dp", None),
        P("expert", "dp", None),
        P("expert", "dp", None),
    )
    return jax.shard_map(shards, mesh=mesh, in_specs=in_specs, out_specs=out_specs, check_vma=False)
```

```python
import functools

import jax
import jax.numpy as jnp
from jax import lax
from jax.experimental import pallas as pl
from jax.experimental.pallas import tpu as pltpu
from jax.sharding import PartitionSpec as P

F32 = jnp.float32
BF16 = jnp.bfloat16
MAIN = 8
QUARTERS = 4
LANES = 256
MIB = 1024 * 1024
FREE = pl.CostEstimate(flops=0, bytes_accessed=0, transcendentals=0)


def mm(a, b, dims):
    return lax.dot_general(a, b, (dims, ((), ())), preferred_element_type=F32)


NN = ((1,), (0,))
NT = ((1,), (1,))
TN = ((0,), (0,))


def params(mib):
    return pltpu.CompilerParams(vmem_limit_bytes=mib * MIB)


def iota(shape, dim):
    return lax.broadcasted_iota(jnp.int32, shape, dim)


def as_col(row):
    tall = jnp.broadcast_to(row.astype(F32), (128, row.shape[1]))
    return jnp.transpose(tall)[:, 0:1].astype(jnp.int32)


def in_hbm(x):
    return pltpu.with_memory_space_constraint(x, pltpu.HBM)


def mask(cond):
    return jnp.where(cond, 1.0, 0.0).astype(BF16)


def pack_kernel(rows, peers, exp_hbm, tok_hbm, gout_hbm, out_hbm, exp_ref, src, out, sem_exp, sem_in, sem_out):
    expert = pltpu.make_async_copy(exp_hbm, exp_ref, sem_exp)
    expert.start()
    width = tok_hbm.shape[1]
    part = width // QUARTERS
    both = width + part
    loads = []
    for k, hbm in enumerate((tok_hbm, gout_hbm)):
        for q in range(QUARTERS):
            cols = pl.ds(q * part, part)
            copy = pltpu.make_async_copy(hbm.at[:, cols], src.at[k, :, cols], sem_in.at[k * QUARTERS + q])
            copy.start()
            loads.append(copy)
    expert.wait()
    row = exp_ref[...]
    earlier = (as_col(row) == row) & (iota((rows, rows), 0) < iota((rows, rows), 1))
    rank = jnp.sum(jnp.where(earlier, 1.0, 0.0), axis=0, keepdims=True).astype(jnp.int32)
    slots = peers * MAIN
    r = iota((slots, rows), 0)
    here = (r >> 3) == row
    whole = mask(here & ((r & 7) == rank))
    late = here & (((r >> 2) & 1) + MAIN == rank)
    late = [mask(late & ((r & 3) == q)) for q in range(QUARTERS)]
    stores = []

    def store(lo, size):
        cols = pl.ds(lo, size)
        copy = pltpu.make_async_copy(out.at[:, cols], out_hbm.at[:, cols], sem_out.at[len(stores)])
        copy.start()
        stores.append(copy)

    for k in range(2):
        at = k * both
        tail = jnp.zeros((slots, part), F32)
        for q in range(QUARTERS):
            loads[k * QUARTERS + q].wait()
            cols = src[k, :, q * part : (q + 1) * part]
            out[:, at + q * part : at + (q + 1) * part] = mm(whole, cols, NN).astype(BF16)
            store(at + q * part, part)
            tail += mm(late[q], cols, NN)
        out[:, at + width : at + both] = tail.astype(BF16)
        store(at + width, part)
    for copy in stores:
        copy.wait()


def pack(expert_row, tokens, grad_out, peers):
    rows, width = tokens.shape
    both = width + width // QUARTERS
    slots = peers * MAIN
    hbm = pl.BlockSpec(memory_space=pltpu.HBM)
    return pl.pallas_call(
        functools.partial(pack_kernel, rows, peers),
        in_specs=[hbm, hbm, hbm],
        out_specs=hbm,
        out_shape=pltpu.HBM((slots, 2 * both), BF16),
        scratch_shapes=[
            pltpu.VMEM((1, rows), jnp.int32),
            pltpu.VMEM((2, rows, width), BF16),
            pltpu.VMEM((slots, 2 * both), BF16),
            pltpu.SemaphoreType.DMA,
            pltpu.SemaphoreType.DMA((2 * QUARTERS,)),
            pltpu.SemaphoreType.DMA((2 * QUARTERS + 2,)),
        ],
        compiler_params=params(12),
        cost_estimate=FREE,
        name="pack",
    )(in_hbm(expert_row), in_hbm(tokens), in_hbm(grad_out))


def fetch_kernel(src, dst, sem):
    copy = pltpu.make_async_copy(src, dst, sem)
    copy.start()
    copy.wait()


def fetch(array):
    return pl.pallas_call(
        fetch_kernel,
        in_specs=[pl.BlockSpec(memory_space=pltpu.HBM)],
        out_specs=pl.BlockSpec(memory_space=pltpu.VMEM),
        out_shape=pltpu.VMEM(array.shape, array.dtype),
        scratch_shapes=[pltpu.SemaphoreType.DMA],
        compiler_params=params(2),
        cost_estimate=FREE,
        name="fetch",
    )(in_hbm(array))


def unpack_kernel(rows, peers, exp_ref, back_ref, mixed_ref, gtok_ref):
    row = exp_ref[...]
    col = as_col(row)
    earlier = (col == row) & (iota((rows, rows), 1) < iota((rows, rows), 0))
    rank = jnp.sum(jnp.where(earlier, 1.0, 0.0), axis=1, keepdims=True).astype(jnp.int32)
    slots = peers * MAIN
    r = iota((rows, slots), 1)
    here = (r >> 3) == col
    whole = mask(here & ((r & 7) == rank))
    late = here & (((r >> 2) & 1) + MAIN == rank)
    part = mixed_ref.shape[1] // QUARTERS
    both = part * (QUARTERS + 1)
    for k, dst in enumerate((mixed_ref, gtok_ref)):
        at = k * both
        tail = back_ref[:, at + QUARTERS * part : at + both]
        for q in range(QUARTERS):
            got = mm(whole, back_ref[:, at + q * part : at + (q + 1) * part], NN)
            got += mm(mask(late & ((r & 3) == q)), tail, NN)
            dst[:, q * part : (q + 1) * part] = got.astype(BF16)


def unpack(expert_row, back, width, peers):
    rows = expert_row.shape[1]
    out = jax.ShapeDtypeStruct((rows, width), BF16)
    return pl.pallas_call(
        functools.partial(unpack_kernel, rows, peers),
        out_shape=(out, out),
        compiler_params=params(12),
        cost_estimate=FREE,
        name="unpack",
    )(expert_row, back)


def grad_block(groups, scale, z, x_ref, dy_ref, cut_ref, gg_ref, gu_ref, a_ref, b_ref):
    rows = x_ref.shape[1] // groups
    half = rows // 2
    at = z % groups
    x = x_ref[:, pl.ds(pl.multiple_of(at * rows, 128), rows)]

    def put(ref, base, value):
        n = value.shape[0]
        for c in range(value.shape[1] // LANES):
            ref[base + c * n : base + (c + 1) * n, :] = value[:, c * LANES : (c + 1) * LANES]
        return base + n * (value.shape[1] // LANES)

    if a_ref is not None and b_ref is not None:
        up = (mm(x, gu_ref[...], TN) * scale).astype(BF16)
        upper, lower = up[:half], up[half:]
    elif a_ref is not None:
        upper = (mm(x[:, :half], gu_ref[...], TN) * scale).astype(BF16)
    else:
        lower = (mm(x[:, half:], gu_ref[...], TN) * scale).astype(BF16)
    if a_ref is not None:
        down = (mm(cut_ref[at], dy_ref[...], TN) * scale).astype(BF16)
        put(a_ref, put(a_ref, 0, down), upper)
    if b_ref is not None:
        gate = (mm(x, gg_ref[...], TN) * scale).astype(BF16)
        put(b_ref, put(b_ref, 0, gate), lower)


def hidden_kernel(
    groups, tile, scale, z_ref, recv_hbm, wg_ref, wu_hbm, wd_hbm,
    x_ref, dy_ref, act_ref, cut_ref, gg_ref, gu_ref, a4_hbm, b4_hbm, b3_hbm, a5_hbm,
    recv_ref, wu_ref, wd_ref, gate_ref, up_ref, a4, b4, b3, a5, sem_x, sem_dy, sem_u, sem_d, sem_out,
):
    slots = recv_ref.shape[0]
    width, inner = wg_ref.shape
    part = width // QUARTERS
    both = width + part
    tails = slots // QUARTERS
    tiles = [slice(lo, lo + tile) for lo in range(0, inner, tile)]
    halves = [(slice(None), slice(0, both)), (slice(None), slice(both, 2 * both))]
    load_x = pltpu.make_async_copy(recv_hbm.at[halves[0]], recv_ref.at[halves[0]], sem_x)
    load_dy = pltpu.make_async_copy(recv_hbm.at[halves[1]], recv_ref.at[halves[1]], sem_dy)
    load_u = pltpu.make_async_copy(wu_hbm, wu_ref, sem_u)
    load_d = pltpu.make_async_copy(wd_hbm, wd_ref, sem_d)
    load_x.start()
    load_u.start()
    load_dy.start()
    load_d.start()
    picks = [
        mask(iota((tails, slots), 1) == iota((tails, slots), 0) * QUARTERS + q) for q in range(QUARTERS)
    ]

    def spread(k, dst):
        at = k * both
        dst[0:slots, :] = recv_ref[:, at : at + width]
        tail = recv_ref[:, at + width : at + both]
        for q in range(QUARTERS):
            dst[slots : slots + tails, q * part : (q + 1) * part] = mm(picks[q], tail, NN).astype(BF16)

    load_x.wait()
    spread(0, x_ref)
    for cols in tiles:
        gate_ref[:, cols] = mm(x_ref[...], wg_ref[:, cols], NN)
    load_u.wait()
    for cols in tiles:
        up_ref[:, cols] = mm(x_ref[...], wu_ref[:, cols], NN)
    load_dy.wait()
    spread(1, dy_ref)
    load_d.wait()
    for cols in tiles:
        gate, up = gate_ref[:, cols], up_ref[:, cols]
        grad_act = mm(dy_ref[...], wd_ref[cols, :], NT)
        sig = jax.nn.sigmoid(gate)
        swish = gate * sig
        act_ref[:, cols] = (swish * up).astype(BF16)
        gg_ref[:, cols] = (grad_act * up * sig * (1.0 + gate * (1.0 - sig))).astype(BF16)
        gu_ref[:, cols] = (grad_act * swish).astype(BF16)
    each = inner // groups
    for k in range(groups):
        cut_ref[k] = act_ref[:, k * each : (k + 1) * each]
    far = groups // 2
    z = z_ref[0]
    stores = []

    def store(src, dst):
        stores.append(pltpu.make_async_copy(src, dst, sem_out.at[len(stores)]))
        stores[-1].start()

    grad_block(groups, scale, z + far, x_ref, dy_ref, cut_ref, gg_ref, gu_ref, a4, b4)
    store(a4, a4_hbm)
    store(b4, b4_hbm)
    grad_block(groups, scale, z + far - 1, x_ref, dy_ref, cut_ref, gg_ref, gu_ref, None, b3)
    store(b3, b3_hbm)
    grad_block(groups, scale, z + far + 1, x_ref, dy_ref, cut_ref, gg_ref, gu_ref, a5, None)
    store(a5, a5_hbm)
    for copy in stores:
        copy.wait()


def hidden(z, recv, wg, wu, wd, scale, groups, tile=256):
    slots = recv.shape[0]
    width, inner = wg.shape
    total = slots + slots // QUARTERS
    shapes = [(total, width)] * 2 + [(total, inner), (groups, total, inner // groups)] + [(total, inner)] * 2
    leaving = (3 * width * inner // (2 * groups * LANES), LANES)
    vmem = pl.BlockSpec(memory_space=pltpu.VMEM)
    hbm = pl.BlockSpec(memory_space=pltpu.HBM)
    return pl.pallas_call(
        functools.partial(hidden_kernel, groups, tile, scale),
        in_specs=[pl.BlockSpec(memory_space=pltpu.SMEM), hbm, vmem, hbm, hbm],
        out_specs=[vmem] * len(shapes) + [hbm] * 4,
        out_shape=[jax.ShapeDtypeStruct(s, BF16) for s in shapes] + [pltpu.HBM(leaving, BF16)] * 4,
        scratch_shapes=[
            pltpu.VMEM(recv.shape, BF16),
            pltpu.VMEM(wu.shape, BF16),
            pltpu.VMEM(wd.shape, BF16),
            pltpu.VMEM((total, inner), F32),
            pltpu.VMEM((total, inner), F32),
        ]
        + [pltpu.VMEM(leaving, BF16)] * 4
        + [pltpu.SemaphoreType.DMA] * 4
        + [pltpu.SemaphoreType.DMA((4,))],
        compiler_params=params(24),
        cost_estimate=pl.CostEstimate(
            flops=6 * total * width * inner, bytes_accessed=8 * width * inner, transcendentals=total * inner
        ),
        name="hidden",
    )(z, in_hbm(recv), wg, in_hbm(wu), in_hbm(wd))


def near_kernel(groups, scale, z_ref, cut_ref, x_ref, dy_ref, gg_ref, gu_ref, *refs):
    count = groups - 1
    outs, (a_ref, b_ref, sems) = refs[: 2 * (count - 1)], refs[2 * (count - 1) :]
    copies = []
    for i in range(count):
        z = z_ref[0] + groups // 2 + 1 + i
        a = a_ref.at[i] if i > 0 else None
        b = b_ref.at[i] if i < count - 1 else None
        grad_block(groups, scale, z, x_ref, dy_ref, cut_ref, gg_ref, gu_ref, a, b)
        for ref, out in ((a, i - 1), (b, count - 1 + i)):
            if ref is not None:
                copies.append(pltpu.make_async_copy(ref, outs[out], sems.at[len(copies)]))
                copies[-1].start()
    for copy in copies:
        copy.wait()


def near_blocks(z, cut, x, dy, gg, gu, scale):
    groups, total, each = cut.shape
    width = x.shape[1]
    inner = gg.shape[1]
    vmem = pl.BlockSpec(memory_space=pltpu.VMEM)
    hbm = pl.BlockSpec(memory_space=pltpu.HBM)
    one = (3 * width * inner // (2 * groups * LANES), LANES)
    count = 2 * (groups - 2)
    outs = pl.pallas_call(
        functools.partial(near_kernel, groups, scale),
        in_specs=[pl.BlockSpec(memory_space=pltpu.SMEM)] + [vmem] * 5,
        out_specs=[hbm] * count,
        out_shape=[pltpu.HBM(one, BF16)] * count,
        scratch_shapes=[pltpu.VMEM((groups - 1, *one), BF16)] * 2 + [pltpu.SemaphoreType.DMA((count,))],
        compiler_params=params(16),
        cost_estimate=pl.CostEstimate(
            flops=6 * total * width * inner, bytes_accessed=6 * width * inner, transcendentals=0
        ),
        name="near_blocks",
    )(z, cut, x, dy, gg, gu)
    far = groups // 2
    a = {d: outs[d + far - 2] for d in range(2 - far, far)}
    b = {d: outs[groups - 2 + d + far - 1] for d in range(1 - far, far - 1)}
    return a, b


def almost_kernel(own_a, own_b, al_any, br_any, pa, pb, oa, ob, al, br, sems):
    pairs = ((own_a, oa), (al_any, al), (own_b, ob), (br_any, br))
    loads = [pltpu.make_async_copy(src, dst, sems.at[n]) for n, (src, dst) in enumerate(pairs)]
    for copy in loads:
        copy.start()
    for copy in loads:
        copy.wait()
    pa[...] = oa[...].astype(F32) + al[...].astype(F32)
    pb[...] = ob[...].astype(F32) + br[...].astype(F32)


def almost(own_a, own_b, al, br):
    vmem = pl.BlockSpec(memory_space=pltpu.VMEM)
    return pl.pallas_call(
        almost_kernel,
        in_specs=[pl.BlockSpec(memory_space=pl.ANY)] * 4,
        out_specs=[vmem] * 2,
        out_shape=[pltpu.VMEM(al.shape, F32)] * 2,
        scratch_shapes=[pltpu.VMEM(al.shape, BF16)] * 4 + [pltpu.SemaphoreType.DMA((4,))],
        compiler_params=params(6),
        cost_estimate=FREE,
        name="almost",
    )(in_hbm(own_a), in_hbm(own_b), al, br)


def finish_kernel(after, pa, pb, ar_any, bl_any, down_hbm, gate_hbm, up_hbm, ar, bl, down, gate, up, sem_in, sem_out):
    loads = [
        pltpu.make_async_copy(src, dst, sem_in.at[n]) for n, (src, dst) in enumerate(((ar_any, ar), (bl_any, bl)))
    ]
    for copy in loads:
        copy.start()
    half = up.shape[0] // 2
    stores = []

    def take(part, moved, base, dst):
        rows = dst.shape[0]
        for c in range(dst.shape[1] // LANES):
            at = slice(base + c * rows, base + (c + 1) * rows)
            dst[:, c * LANES : (c + 1) * LANES] = (part[at, :] + moved[at, :].astype(F32)).astype(BF16)
        return base + rows * (dst.shape[1] // LANES)

    def store(src, dst):
        stores.append(pltpu.make_async_copy(src, dst, sem_out.at[len(stores)]))
        stores[-1].start()

    loads[0].wait()
    base = take(pa, ar, 0, down)
    store(down, down_hbm)
    take(pa, ar, base, up.at[:half])
    store(up.at[:half], up_hbm.at[:half])
    loads[1].wait()
    base = take(pb, bl, 0, gate)
    store(gate, gate_hbm)
    take(pb, bl, base, up.at[half:])
    store(up.at[half:], up_hbm.at[half:])
    for copy in stores:
        copy.wait()


def finish(after, sums, ar, bl, groups, width, inner):
    vmem = pl.BlockSpec(memory_space=pltpu.VMEM)
    hbm = pl.BlockSpec(memory_space=pltpu.HBM)
    anywhere = pl.BlockSpec(memory_space=pl.ANY)
    shapes = [(inner // groups, width), (width // groups, inner), (width // groups, inner)]
    return pl.pallas_call(
        finish_kernel,
        in_specs=[anywhere, vmem, vmem, anywhere, anywhere],
        out_specs=[hbm] * 3,
        out_shape=[pltpu.HBM(s, BF16) for s in shapes],
        scratch_shapes=[pltpu.VMEM(ar.shape, BF16)] * 2
        + [pltpu.VMEM(s, BF16) for s in shapes]
        + [pltpu.SemaphoreType.DMA((2,)), pltpu.SemaphoreType.DMA((4,))],
        compiler_params=params(6),
        cost_estimate=FREE,
        name="finish",
    )(in_hbm(after), *sums, ar, bl)


def rows_kernel(
    after, act_ref, gg_ref, gu_ref, wg_hbm, wu_hbm, wd_hbm, out_hbm, wg_ref, wu_ref, wd_ref, out, sem_in, sem_out
):
    slots = out.shape[0]
    width = wg_ref.shape[0]
    part = width // QUARTERS
    both = width + part
    tails = slots // QUARTERS
    loads = []
    for q in range(QUARTERS):
        cut = slice(q * part, (q + 1) * part)
        where = ((wd_hbm, wd_ref, (slice(None), cut)), (wg_hbm, wg_ref, (cut,)), (wu_hbm, wu_ref, (cut,)))
        for n, (src, dst, at) in enumerate(where):
            copy = pltpu.make_async_copy(src.at[at], dst.at[at], sem_in.at[q * 3 + n])
            copy.start()
            loads.append(copy)
    stores = []

    def store(lo):
        cols = pl.ds(lo, part)
        copy = pltpu.make_async_copy(out.at[:, cols], out_hbm.at[:, cols], sem_out.at[len(stores)])
        copy.start()
        stores.append(copy)

    tail = [jnp.zeros((slots, part), F32) for _ in range(2)]
    for q in range(QUARTERS):
        cut = slice(q * part, (q + 1) * part)
        pick = mask(iota((slots, tails), 0) == iota((slots, tails), 1) * QUARTERS + q)
        for k in range(2):
            if k == 0:
                loads[q * 3].wait()
                val = mm(act_ref[...], wd_ref[:, cut], NN).astype(BF16)
            else:
                loads[q * 3 + 1].wait()
                loads[q * 3 + 2].wait()
                val = (mm(gg_ref[...], wg_ref[cut, :], NT) + mm(gu_ref[...], wu_ref[cut, :], NT)).astype(BF16)
            lo = k * both + q * part
            out[:, lo : lo + part] = val[0:slots, :]
            store(lo)
            tail[k] += mm(pick, val[slots : slots + tails, :], NN)
    for k in range(2):
        lo = k * both + width
        out[:, lo : lo + part] = tail[k].astype(BF16)
        store(lo)
    for copy in stores:
        copy.wait()


def rows_back(after, act, gg, gu, wg, wu, wd):
    total, inner = act.shape
    width = wg.shape[0]
    slots = total * QUARTERS // (QUARTERS + 1)
    out = (slots, 2 * (width + width // QUARTERS))
    vmem = pl.BlockSpec(memory_space=pltpu.VMEM)
    hbm = pl.BlockSpec(memory_space=pltpu.HBM)
    return pl.pallas_call(
        rows_kernel,
        in_specs=[pl.BlockSpec(memory_space=pl.ANY), vmem, vmem, vmem, hbm, hbm, hbm],
        out_specs=hbm,
        out_shape=pltpu.HBM(out, BF16),
        scratch_shapes=[
            pltpu.VMEM(wg.shape, BF16),
            pltpu.VMEM(wu.shape, BF16),
            pltpu.VMEM(wd.shape, BF16),
            pltpu.VMEM(out, BF16),
            pltpu.SemaphoreType.DMA((3 * QUARTERS,)),
            pltpu.SemaphoreType.DMA((2 * QUARTERS + 2,)),
        ],
        compiler_params=params(20),
        cost_estimate=pl.CostEstimate(
            flops=6 * total * width * inner, bytes_accessed=6 * width * inner, transcendentals=0
        ),
        name="rows_back",
    )(in_hbm(after), act, gg, gu, in_hbm(wg), in_hbm(wu), in_hbm(wd))


def step_kernel(after, own_r, own_l, r_any, l_any, out_r, out_l, o_r, o_l, r, l, sems):
    pairs = ((own_r, o_r), (r_any, r), (own_l, o_l), (l_any, l))
    loads = [pltpu.make_async_copy(src, dst, sems.at[n]) for n, (src, dst) in enumerate(pairs)]
    for copy in loads:
        copy.start()
    stores = []
    for n, (own, moved, out) in enumerate(((o_r, r, out_r), (o_l, l, out_l))):
        for copy in loads[2 * n : 2 * n + 2]:
            copy.wait()
        own[...] = (own[...].astype(F32) + moved[...].astype(F32)).astype(BF16)
        stores.append(pltpu.make_async_copy(own, out, sems.at[4 + n]))
        stores[n].start()
    for copy in stores:
        copy.wait()


def ring_step(after, own_r, own_l, r, l):
    hbm = pl.BlockSpec(memory_space=pltpu.HBM)
    return pl.pallas_call(
        step_kernel,
        in_specs=[pl.BlockSpec(memory_space=pl.ANY)] * 5,
        out_specs=[hbm] * 2,
        out_shape=[pltpu.HBM(r.shape, BF16)] * 2,
        scratch_shapes=[pltpu.VMEM(r.shape, BF16)] * 4 + [pltpu.SemaphoreType.DMA((6,))],
        compiler_params=params(6),
        cost_estimate=pl.CostEstimate(flops=10**10, bytes_accessed=0, transcendentals=0),
        name="ring_step",
    )(in_hbm(after), in_hbm(own_r), in_hbm(own_l), r, l)


def ring_sums(first, rest, groups):
    right = [(i, (i + 1) % groups) for i in range(groups)]
    left = [(i, (i - 1) % groups) for i in range(groups)]
    far = groups // 2
    send = lambda r, l: (lax.ppermute(r, "dp", right), lax.ppermute(l, "dp", left))
    a4, b4, b3, a5 = first
    a, b = 0, 1
    moving = [send(a4, b4), send(b3, a5)]
    after = None
    for n in range(2, 2 * far - 1):
        i, j = (a, b) if n % 2 == 0 else (b, a)
        d = far - (n + 1) // 2
        r, l = moving[n - 2]
        after = ring_step(rest[a][0] if after is None else after[0], rest[i][d], rest[j][-d], r, l)
        moving.append(send(*after))
    br, al = moving[-2]
    return almost(rest[a][0], rest[b][0], al, br), *moving[-1]


def shards(tokens, expert_of, w_gate, w_up, w_down, grad_out):
    rows, width = tokens.shape
    peers = lax.axis_size("expert")
    groups = lax.axis_size("dp")
    wg, wu, wd = w_gate[0], w_up[0], w_down[0]
    scale = float(rows * groups) ** (-0.5)

    def exchange(packed):
        swapped = lax.all_to_all(
            packed.reshape(peers, MAIN, -1), "expert", split_axis=0, concat_axis=0, tiled=True
        )
        return swapped.reshape(peers * MAIN, -1)

    expert_row = expert_of.reshape(1, rows)
    z = lax.axis_index("dp").astype(jnp.int32).reshape(1)
    recv = exchange(pack(expert_row, tokens, grad_out, peers))
    x, dy, act, cut, gg, gu, *first = hidden(z, recv, fetch(wg), wu, wd, scale, groups)
    rest = near_blocks(z, cut, x, dy, gg, gu, scale)
    back = exchange(rows_back(rest[0][0], act, gg, gu, wg, wu, wd))
    sums, ar, bl = ring_sums(first, rest, groups)
    mixed, grad_tokens = unpack(expert_row, back, width, peers)
    grad_down, grad_gate, grad_up = finish(mixed, sums, ar, bl, groups, width, wg.shape[1])
    return mixed, grad_tokens, grad_gate[None], grad_up[None], grad_down[None]


def solution(mesh):
    in_specs = (
        P(("dp", "expert"), None),
        P(("dp", "expert"), None),
        P("expert", None, None),
        P("expert", None, None),
        P("expert", None, None),
        P(("dp", "expert"), None),
    )
    out_specs = (
        P(("dp", "expert"), None),
        P(("dp", "expert"), None),
        P("expert", "dp", None),
        P("expert", "dp", None),
        P("expert", "dp", None),
    )
    return jax.shard_map(shards, mesh=mesh, in_specs=in_specs, out_specs=out_specs, check_vma=False)
```

```python
import functools

import jax
import jax.numpy as jnp
from jax import lax
from jax.experimental import pallas as pl
from jax.experimental.pallas import tpu as pltpu
from jax.sharding import PartitionSpec as P

F32 = jnp.float32
BF16 = jnp.bfloat16
MAIN = 8
QUARTERS = 4
LANES = 256
MIB = 1024 * 1024
FREE = pl.CostEstimate(flops=0, bytes_accessed=0, transcendentals=0)


def mm(a, b, dims):
    return lax.dot_general(a, b, (dims, ((), ())), preferred_element_type=F32)


NN = ((1,), (0,))
NT = ((1,), (1,))
TN = ((0,), (0,))


def params(mib):
    return pltpu.CompilerParams(vmem_limit_bytes=mib * MIB)


def iota(shape, dim):
    return lax.broadcasted_iota(jnp.int32, shape, dim)


def as_col(row):
    tall = jnp.broadcast_to(row.astype(F32), (128, row.shape[1]))
    return jnp.transpose(tall)[:, 0:1].astype(jnp.int32)


def in_hbm(x):
    return pltpu.with_memory_space_constraint(x, pltpu.HBM)


def mask(cond):
    return jnp.where(cond, 1.0, 0.0).astype(BF16)


def pack_kernel(rows, peers, exp_hbm, tok_hbm, gout_hbm, out_hbm, exp_ref, src, out, sem_exp, sem_in, sem_out):
    expert = pltpu.make_async_copy(exp_hbm, exp_ref, sem_exp)
    expert.start()
    width = tok_hbm.shape[1]
    part = width // QUARTERS
    both = width + part
    loads = []
    for k, hbm in enumerate((tok_hbm, gout_hbm)):
        copy = pltpu.make_async_copy(hbm, src.at[k], sem_in.at[k])
        copy.start()
        loads.append(copy)
    expert.wait()
    row = exp_ref[...]
    earlier = (as_col(row) == row) & (iota((rows, rows), 0) < iota((rows, rows), 1))
    rank = jnp.sum(jnp.where(earlier, 1.0, 0.0), axis=0, keepdims=True).astype(jnp.int32)
    slots = peers * MAIN
    r = iota((slots, rows), 0)
    here = (r >> 3) == row
    whole = mask(here & ((r & 7) == rank))
    late = here & (((r >> 2) & 1) + MAIN == rank)
    late = [mask(late & ((r & 3) == q)) for q in range(QUARTERS)]
    stores = []

    def store(lo, size):
        cols = pl.ds(lo, size)
        copy = pltpu.make_async_copy(out.at[:, cols], out_hbm.at[:, cols], sem_out.at[len(stores)])
        copy.start()
        stores.append(copy)

    for k in range(2):
        at = k * both
        tail = jnp.zeros((slots, part), F32)
        loads[k].wait()
        for q in range(QUARTERS):
            cols = src[k, :, q * part : (q + 1) * part]
            out[:, at + q * part : at + (q + 1) * part] = mm(whole, cols, NN).astype(BF16)
            store(at + q * part, part)
            tail += mm(late[q], cols, NN)
        out[:, at + width : at + both] = tail.astype(BF16)
        store(at + width, part)
    for copy in stores:
        copy.wait()


def pack(expert_row, tokens, grad_out, peers):
    rows, width = tokens.shape
    both = width + width // QUARTERS
    slots = peers * MAIN
    hbm = pl.BlockSpec(memory_space=pltpu.HBM)
    return pl.pallas_call(
        functools.partial(pack_kernel, rows, peers),
        in_specs=[hbm, hbm, hbm],
        out_specs=hbm,
        out_shape=pltpu.HBM((slots, 2 * both), BF16),
        scratch_shapes=[
            pltpu.VMEM((1, rows), jnp.int32),
            pltpu.VMEM((2, rows, width), BF16),
            pltpu.VMEM((slots, 2 * both), BF16),
            pltpu.SemaphoreType.DMA,
            pltpu.SemaphoreType.DMA((2 * QUARTERS,)),
            pltpu.SemaphoreType.DMA((2 * QUARTERS + 2,)),
        ],
        compiler_params=params(12),
        cost_estimate=FREE,
        name="pack",
    )(in_hbm(expert_row), in_hbm(tokens), in_hbm(grad_out))


def fetch_kernel(src, dst, sem):
    copy = pltpu.make_async_copy(src, dst, sem)
    copy.start()
    copy.wait()


def fetch(array):
    return pl.pallas_call(
        fetch_kernel,
        in_specs=[pl.BlockSpec(memory_space=pltpu.HBM)],
        out_specs=pl.BlockSpec(memory_space=pltpu.VMEM),
        out_shape=pltpu.VMEM(array.shape, array.dtype),
        scratch_shapes=[pltpu.SemaphoreType.DMA],
        compiler_params=params(2),
        cost_estimate=FREE,
        name="fetch",
    )(in_hbm(array))


def unpack_kernel(rows, peers, exp_ref, back_ref, mixed_ref, gtok_ref):
    row = exp_ref[...]
    col = as_col(row)
    earlier = (col == row) & (iota((rows, rows), 1) < iota((rows, rows), 0))
    rank = jnp.sum(jnp.where(earlier, 1.0, 0.0), axis=1, keepdims=True).astype(jnp.int32)
    slots = peers * MAIN
    r = iota((rows, slots), 1)
    here = (r >> 3) == col
    whole = mask(here & ((r & 7) == rank))
    late = here & (((r >> 2) & 1) + MAIN == rank)
    part = mixed_ref.shape[1] // QUARTERS
    both = part * (QUARTERS + 1)
    for k, dst in enumerate((mixed_ref, gtok_ref)):
        at = k * both
        tail = back_ref[:, at + QUARTERS * part : at + both]
        for q in range(QUARTERS):
            got = mm(whole, back_ref[:, at + q * part : at + (q + 1) * part], NN)
            got += mm(mask(late & ((r & 3) == q)), tail, NN)
            dst[:, q * part : (q + 1) * part] = got.astype(BF16)


def unpack(expert_row, back, width, peers):
    rows = expert_row.shape[1]
    out = jax.ShapeDtypeStruct((rows, width), BF16)
    return pl.pallas_call(
        functools.partial(unpack_kernel, rows, peers),
        out_shape=(out, out),
        compiler_params=params(12),
        cost_estimate=FREE,
        name="unpack",
    )(expert_row, back)


def grad_block(groups, scale, z, x_ref, dy_ref, cut_ref, gg_ref, gu_ref, a_ref, b_ref):
    rows = x_ref.shape[1] // groups
    half = rows // 2
    at = z % groups
    x = x_ref[:, pl.ds(pl.multiple_of(at * rows, 128), rows)]

    def put(ref, base, value):
        n = value.shape[0]
        for c in range(value.shape[1] // LANES):
            ref[base + c * n : base + (c + 1) * n, :] = value[:, c * LANES : (c + 1) * LANES]
        return base + n * (value.shape[1] // LANES)

    if a_ref is not None and b_ref is not None:
        up = (mm(x, gu_ref[...], TN) * scale).astype(BF16)
        upper, lower = up[:half], up[half:]
    elif a_ref is not None:
        upper = (mm(x[:, :half], gu_ref[...], TN) * scale).astype(BF16)
    else:
        lower = (mm(x[:, half:], gu_ref[...], TN) * scale).astype(BF16)
    if a_ref is not None:
        down = (mm(cut_ref[at], dy_ref[...], TN) * scale).astype(BF16)
        put(a_ref, put(a_ref, 0, down), upper)
    if b_ref is not None:
        gate = (mm(x, gg_ref[...], TN) * scale).astype(BF16)
        put(b_ref, put(b_ref, 0, gate), lower)


def hidden_kernel(
    groups, tile, scale, z_ref, recv_hbm, wg_ref, wu_hbm, wd_hbm,
    x_ref, dy_ref, act_ref, cut_ref, gg_ref, gu_ref, a4_hbm, b4_hbm, b3_hbm, a5_hbm,
    recv_ref, wu_ref, wd_ref, gate_ref, up_ref, a4, b4, b3, a5, sem_x, sem_dy, sem_u, sem_d, sem_out,
):
    slots = recv_ref.shape[0]
    width, inner = wg_ref.shape
    part = width // QUARTERS
    both = width + part
    tails = slots // QUARTERS
    tiles = [slice(lo, lo + tile) for lo in range(0, inner, tile)]
    halves = [(slice(None), slice(0, both)), (slice(None), slice(both, 2 * both))]
    load_x = pltpu.make_async_copy(recv_hbm.at[halves[0]], recv_ref.at[halves[0]], sem_x)
    load_dy = pltpu.make_async_copy(recv_hbm.at[halves[1]], recv_ref.at[halves[1]], sem_dy)
    load_u = pltpu.make_async_copy(wu_hbm, wu_ref, sem_u)
    load_d = pltpu.make_async_copy(wd_hbm, wd_ref, sem_d)
    load_x.start()
    load_u.start()
    load_dy.start()
    load_d.start()
    picks = [
        mask(iota((tails, slots), 1) == iota((tails, slots), 0) * QUARTERS + q) for q in range(QUARTERS)
    ]

    def spread(k, dst):
        at = k * both
        dst[0:slots, :] = recv_ref[:, at : at + width]
        tail = recv_ref[:, at + width : at + both]
        for q in range(QUARTERS):
            dst[slots : slots + tails, q * part : (q + 1) * part] = mm(picks[q], tail, NN).astype(BF16)

    load_x.wait()
    spread(0, x_ref)
    for cols in tiles:
        gate_ref[:, cols] = mm(x_ref[...], wg_ref[:, cols], NN)
    load_u.wait()
    for cols in tiles:
        up_ref[:, cols] = mm(x_ref[...], wu_ref[:, cols], NN)
    load_dy.wait()
    spread(1, dy_ref)
    load_d.wait()
    for cols in tiles:
        gate, up = gate_ref[:, cols], up_ref[:, cols]
        grad_act = mm(dy_ref[...], wd_ref[cols, :], NT)
        sig = jax.nn.sigmoid(gate)
        swish = gate * sig
        act_ref[:, cols] = (swish * up).astype(BF16)
        gg_ref[:, cols] = (grad_act * up * sig * (1.0 + gate * (1.0 - sig))).astype(BF16)
        gu_ref[:, cols] = (grad_act * swish).astype(BF16)
    each = inner // groups
    for k in range(groups):
        cut_ref[k] = act_ref[:, k * each : (k + 1) * each]
    far = groups // 2
    z = z_ref[0]
    stores = []

    def store(src, dst):
        stores.append(pltpu.make_async_copy(src, dst, sem_out.at[len(stores)]))
        stores[-1].start()

    grad_block(groups, scale, z + far, x_ref, dy_ref, cut_ref, gg_ref, gu_ref, a4, b4)
    store(a4, a4_hbm)
    store(b4, b4_hbm)
    grad_block(groups, scale, z + far - 1, x_ref, dy_ref, cut_ref, gg_ref, gu_ref, None, b3)
    store(b3, b3_hbm)
    grad_block(groups, scale, z + far + 1, x_ref, dy_ref, cut_ref, gg_ref, gu_ref, a5, None)
    store(a5, a5_hbm)
    for copy in stores:
        copy.wait()


def hidden(z, recv, wg, wu, wd, scale, groups, tile=256):
    slots = recv.shape[0]
    width, inner = wg.shape
    total = slots + slots // QUARTERS
    shapes = [(total, width)] * 2 + [(total, inner), (groups, total, inner // groups)] + [(total, inner)] * 2
    leaving = (3 * width * inner // (2 * groups * LANES), LANES)
    vmem = pl.BlockSpec(memory_space=pltpu.VMEM)
    hbm = pl.BlockSpec(memory_space=pltpu.HBM)
    return pl.pallas_call(
        functools.partial(hidden_kernel, groups, tile, scale),
        in_specs=[pl.BlockSpec(memory_space=pltpu.SMEM), hbm, vmem, hbm, hbm],
        out_specs=[vmem] * len(shapes) + [hbm] * 4,
        out_shape=[jax.ShapeDtypeStruct(s, BF16) for s in shapes] + [pltpu.HBM(leaving, BF16)] * 4,
        scratch_shapes=[
            pltpu.VMEM(recv.shape, BF16),
            pltpu.VMEM(wu.shape, BF16),
            pltpu.VMEM(wd.shape, BF16),
            pltpu.VMEM((total, inner), F32),
            pltpu.VMEM((total, inner), F32),
        ]
        + [pltpu.VMEM(leaving, BF16)] * 4
        + [pltpu.SemaphoreType.DMA] * 4
        + [pltpu.SemaphoreType.DMA((4,))],
        compiler_params=params(24),
        cost_estimate=pl.CostEstimate(
            flops=6 * total * width * inner, bytes_accessed=8 * width * inner, transcendentals=total * inner
        ),
        name="hidden",
    )(z, in_hbm(recv), wg, in_hbm(wu), in_hbm(wd))


def near_kernel(groups, scale, z_ref, cut_ref, x_ref, dy_ref, gg_ref, gu_ref, *refs):
    count = groups - 1
    outs, (a_ref, b_ref, sems) = refs[: 2 * (count - 1)], refs[2 * (count - 1) :]
    copies = []
    for i in range(count):
        z = z_ref[0] + groups // 2 + 1 + i
        a = a_ref.at[i] if i > 0 else None
        b = b_ref.at[i] if i < count - 1 else None
        grad_block(groups, scale, z, x_ref, dy_ref, cut_ref, gg_ref, gu_ref, a, b)
        for ref, out in ((a, i - 1), (b, count - 1 + i)):
            if ref is not None:
                copies.append(pltpu.make_async_copy(ref, outs[out], sems.at[len(copies)]))
                copies[-1].start()
    for copy in copies:
        copy.wait()


def near_blocks(z, cut, x, dy, gg, gu, scale):
    groups, total, each = cut.shape
    width = x.shape[1]
    inner = gg.shape[1]
    vmem = pl.BlockSpec(memory_space=pltpu.VMEM)
    hbm = pl.BlockSpec(memory_space=pltpu.HBM)
    one = (3 * width * inner // (2 * groups * LANES), LANES)
    count = 2 * (groups - 2)
    outs = pl.pallas_call(
        functools.partial(near_kernel, groups, scale),
        in_specs=[pl.BlockSpec(memory_space=pltpu.SMEM)] + [vmem] * 5,
        out_specs=[hbm] * count,
        out_shape=[pltpu.HBM(one, BF16)] * count,
        scratch_shapes=[pltpu.VMEM((groups - 1, *one), BF16)] * 2 + [pltpu.SemaphoreType.DMA((count,))],
        compiler_params=params(16),
        cost_estimate=pl.CostEstimate(
            flops=6 * total * width * inner, bytes_accessed=6 * width * inner, transcendentals=0
        ),
        name="near_blocks",
    )(z, cut, x, dy, gg, gu)
    far = groups // 2
    a = {d: outs[d + far - 2] for d in range(2 - far, far)}
    b = {d: outs[groups - 2 + d + far - 1] for d in range(1 - far, far - 1)}
    return a, b


def almost_kernel(own_a, own_b, al_any, br_any, pa, pb, oa, ob, al, br, sems):
    pairs = ((own_a, oa), (al_any, al), (own_b, ob), (br_any, br))
    loads = [pltpu.make_async_copy(src, dst, sems.at[n]) for n, (src, dst) in enumerate(pairs)]
    for copy in loads:
        copy.start()
    for copy in loads:
        copy.wait()
    pa[...] = oa[...].astype(F32) + al[...].astype(F32)
    pb[...] = ob[...].astype(F32) + br[...].astype(F32)


def almost(own_a, own_b, al, br):
    vmem = pl.BlockSpec(memory_space=pltpu.VMEM)
    return pl.pallas_call(
        almost_kernel,
        in_specs=[pl.BlockSpec(memory_space=pl.ANY)] * 4,
        out_specs=[vmem] * 2,
        out_shape=[pltpu.VMEM(al.shape, F32)] * 2,
        scratch_shapes=[pltpu.VMEM(al.shape, BF16)] * 4 + [pltpu.SemaphoreType.DMA((4,))],
        compiler_params=params(6),
        cost_estimate=FREE,
        name="almost",
    )(in_hbm(own_a), in_hbm(own_b), al, br)


def finish_kernel(after, pa, pb, ar_any, bl_any, down_hbm, gate_hbm, up_hbm, ar, bl, down, gate, up, sem_in, sem_out):
    loads = [
        pltpu.make_async_copy(src, dst, sem_in.at[n]) for n, (src, dst) in enumerate(((ar_any, ar), (bl_any, bl)))
    ]
    for copy in loads:
        copy.start()
    half = up.shape[0] // 2
    stores = []

    def take(part, moved, base, dst):
        rows = dst.shape[0]
        for c in range(dst.shape[1] // LANES):
            at = slice(base + c * rows, base + (c + 1) * rows)
            dst[:, c * LANES : (c + 1) * LANES] = (part[at, :] + moved[at, :].astype(F32)).astype(BF16)
        return base + rows * (dst.shape[1] // LANES)

    def store(src, dst):
        stores.append(pltpu.make_async_copy(src, dst, sem_out.at[len(stores)]))
        stores[-1].start()

    loads[0].wait()
    base = take(pa, ar, 0, down)
    store(down, down_hbm)
    take(pa, ar, base, up.at[:half])
    store(up.at[:half], up_hbm.at[:half])
    loads[1].wait()
    base = take(pb, bl, 0, gate)
    store(gate, gate_hbm)
    take(pb, bl, base, up.at[half:])
    store(up.at[half:], up_hbm.at[half:])
    for copy in stores:
        copy.wait()


def finish(after, sums, ar, bl, groups, width, inner):
    vmem = pl.BlockSpec(memory_space=pltpu.VMEM)
    hbm = pl.BlockSpec(memory_space=pltpu.HBM)
    anywhere = pl.BlockSpec(memory_space=pl.ANY)
    shapes = [(inner // groups, width), (width // groups, inner), (width // groups, inner)]
    return pl.pallas_call(
        finish_kernel,
        in_specs=[anywhere, vmem, vmem, anywhere, anywhere],
        out_specs=[hbm] * 3,
        out_shape=[pltpu.HBM(s, BF16) for s in shapes],
        scratch_shapes=[pltpu.VMEM(ar.shape, BF16)] * 2
        + [pltpu.VMEM(s, BF16) for s in shapes]
        + [pltpu.SemaphoreType.DMA((2,)), pltpu.SemaphoreType.DMA((4,))],
        compiler_params=params(6),
        cost_estimate=FREE,
        name="finish",
    )(in_hbm(after), *sums, ar, bl)


def rows_kernel(
    after, act_ref, gg_ref, gu_ref, wg_hbm, wu_hbm, wd_hbm, out_hbm, wg_ref, wu_ref, wd_ref, out, sem_in, sem_out
):
    slots = out.shape[0]
    width = wg_ref.shape[0]
    part = width // QUARTERS
    both = width + part
    tails = slots // QUARTERS
    loads = []
    for q in range(QUARTERS):
        cut = slice(q * part, (q + 1) * part)
        where = ((wd_hbm, wd_ref, (slice(None), cut)), (wg_hbm, wg_ref, (cut,)), (wu_hbm, wu_ref, (cut,)))
        for n, (src, dst, at) in enumerate(where):
            copy = pltpu.make_async_copy(src.at[at], dst.at[at], sem_in.at[q * 3 + n])
            copy.start()
            loads.append(copy)
    stores = []

    def store(lo):
        cols = pl.ds(lo, part)
        copy = pltpu.make_async_copy(out.at[:, cols], out_hbm.at[:, cols], sem_out.at[len(stores)])
        copy.start()
        stores.append(copy)

    tail = [jnp.zeros((slots, part), F32) for _ in range(2)]
    for q in range(QUARTERS):
        cut = slice(q * part, (q + 1) * part)
        pick = mask(iota((slots, tails), 0) == iota((slots, tails), 1) * QUARTERS + q)
        for k in range(2):
            if k == 0:
                loads[q * 3].wait()
                val = mm(act_ref[...], wd_ref[:, cut], NN).astype(BF16)
            else:
                loads[q * 3 + 1].wait()
                loads[q * 3 + 2].wait()
                val = (mm(gg_ref[...], wg_ref[cut, :], NT) + mm(gu_ref[...], wu_ref[cut, :], NT)).astype(BF16)
            lo = k * both + q * part
            out[:, lo : lo + part] = val[0:slots, :]
            store(lo)
            tail[k] += mm(pick, val[slots : slots + tails, :], NN)
    for k in range(2):
        lo = k * both + width
        out[:, lo : lo + part] = tail[k].astype(BF16)
        store(lo)
    for copy in stores:
        copy.wait()


def rows_back(after, act, gg, gu, wg, wu, wd):
    total, inner = act.shape
    width = wg.shape[0]
    slots = total * QUARTERS // (QUARTERS + 1)
    out = (slots, 2 * (width + width // QUARTERS))
    vmem = pl.BlockSpec(memory_space=pltpu.VMEM)
    hbm = pl.BlockSpec(memory_space=pltpu.HBM)
    return pl.pallas_call(
        rows_kernel,
        in_specs=[pl.BlockSpec(memory_space=pl.ANY), vmem, vmem, vmem, hbm, hbm, hbm],
        out_specs=hbm,
        out_shape=pltpu.HBM(out, BF16),
        scratch_shapes=[
            pltpu.VMEM(wg.shape, BF16),
            pltpu.VMEM(wu.shape, BF16),
            pltpu.VMEM(wd.shape, BF16),
            pltpu.VMEM(out, BF16),
            pltpu.SemaphoreType.DMA((3 * QUARTERS,)),
            pltpu.SemaphoreType.DMA((2 * QUARTERS + 2,)),
        ],
        compiler_params=params(20),
        cost_estimate=pl.CostEstimate(
            flops=6 * total * width * inner, bytes_accessed=6 * width * inner, transcendentals=0
        ),
        name="rows_back",
    )(in_hbm(after), act, gg, gu, in_hbm(wg), in_hbm(wu), in_hbm(wd))


def step_kernel(after, own_r, own_l, r_any, l_any, out_r, out_l, o_r, o_l, r, l, sems):
    pairs = ((own_r, o_r), (r_any, r), (own_l, o_l), (l_any, l))
    loads = [pltpu.make_async_copy(src, dst, sems.at[n]) for n, (src, dst) in enumerate(pairs)]
    for copy in loads:
        copy.start()
    stores = []
    for n, (own, moved, out) in enumerate(((o_r, r, out_r), (o_l, l, out_l))):
        for copy in loads[2 * n : 2 * n + 2]:
            copy.wait()
        own[...] = (own[...].astype(F32) + moved[...].astype(F32)).astype(BF16)
        stores.append(pltpu.make_async_copy(own, out, sems.at[4 + n]))
        stores[n].start()
    for copy in stores:
        copy.wait()


def ring_step(after, own_r, own_l, r, l):
    hbm = pl.BlockSpec(memory_space=pltpu.HBM)
    return pl.pallas_call(
        step_kernel,
        in_specs=[pl.BlockSpec(memory_space=pl.ANY)] * 5,
        out_specs=[hbm] * 2,
        out_shape=[pltpu.HBM(r.shape, BF16)] * 2,
        scratch_shapes=[pltpu.VMEM(r.shape, BF16)] * 4 + [pltpu.SemaphoreType.DMA((6,))],
        compiler_params=params(6),
        cost_estimate=pl.CostEstimate(flops=10**10, bytes_accessed=0, transcendentals=0),
        name="ring_step",
    )(in_hbm(after), in_hbm(own_r), in_hbm(own_l), r, l)


def ring_sums(first, rest, groups):
    right = [(i, (i + 1) % groups) for i in range(groups)]
    left = [(i, (i - 1) % groups) for i in range(groups)]
    far = groups // 2
    send = lambda r, l: (lax.ppermute(r, "dp", right), lax.ppermute(l, "dp", left))
    a4, b4, b3, a5 = first
    a, b = 0, 1
    moving = [send(a4, b4), send(b3, a5)]
    after = None
    for n in range(2, 2 * far - 1):
        i, j = (a, b) if n % 2 == 0 else (b, a)
        d = far - (n + 1) // 2
        r, l = moving[n - 2]
        after = ring_step(rest[a][0] if after is None else after[0], rest[i][d], rest[j][-d], r, l)
        moving.append(send(*after))
    br, al = moving[-2]
    return almost(rest[a][0], rest[b][0], al, br), *moving[-1]


def shards(tokens, expert_of, w_gate, w_up, w_down, grad_out):
    rows, width = tokens.shape
    peers = lax.axis_size("expert")
    groups = lax.axis_size("dp")
    wg, wu, wd = w_gate[0], w_up[0], w_down[0]
    scale = float(rows * groups) ** (-0.5)

    def exchange(packed):
        swapped = lax.all_to_all(
            packed.reshape(peers, MAIN, -1), "expert", split_axis=0, concat_axis=0, tiled=True
        )
        return swapped.reshape(peers * MAIN, -1)

    expert_row = expert_of.reshape(1, rows)
    z = lax.axis_index("dp").astype(jnp.int32).reshape(1)
    recv = exchange(pack(expert_row, tokens, grad_out, peers))
    x, dy, act, cut, gg, gu, *first = hidden(z, recv, fetch(wg), wu, wd, scale, groups)
    rest = near_blocks(z, cut, x, dy, gg, gu, scale)
    back = exchange(rows_back(rest[0][0], act, gg, gu, wg, wu, wd))
    sums, ar, bl = ring_sums(first, rest, groups)
    mixed, grad_tokens = unpack(expert_row, back, width, peers)
    grad_down, grad_gate, grad_up = finish(mixed, sums, ar, bl, groups, width, wg.shape[1])
    return mixed, grad_tokens, grad_gate[None], grad_up[None], grad_down[None]


def solution(mesh):
    in_specs = (
        P(("dp", "expert"), None),
        P(("dp", "expert"), None),
        P("expert", None, None),
        P("expert", None, None),
        P("expert", None, None),
        P(("dp", "expert"), None),
    )
    out_specs = (
        P(("dp", "expert"), None),
        P(("dp", "expert"), None),
        P("expert", "dp", None),
        P("expert", "dp", None),
        P("expert", "dp", None),
    )
    return jax.shard_map(shards, mesh=mesh, in_specs=in_specs, out_specs=out_specs, check_vma=False)
```
